32 devices in a mesh: blk: 16 (over z, y, x), grp: 2 (over core).
Axes of the slice: x: 2, y: 2, z: 4, core: 2. Of those that a mesh axis runs over, the one named last changes fastest.
Arguments:
- x_blocks: bfloat16 [512, 128, 128], P(('blk', 'grp')), may hold values from -0.59765625 to 0.59765625
- pair_left: int32 [16, 2, 16, 12], P('blk', 'grp'), may hold values from 0 to 31
- pair_right: int32 [16, 2, 16, 12], P('blk', 'grp'), may hold values from 0 to 31
- pair_target: int32 [16, 2, 16, 12], P('blk', 'grp'), may hold values from 0 to 3
Outputs:
- c_blocks: bfloat16 [16, 2, 4, 128, 128], P('blk', 'grp')
The draws below stay inside these ranges and needn't reach their ends.
All inputs are finite; a program needn't handle non-finite values.
Results may differ from the reference program's by a relative error of at most 0.001.
Values may be sent and summed in bfloat16 or wider, within the bound.
A program may use at most 64 MiB of HBM per device.

```python
import jax
import jax.numpy as jnp
from jax import lax

BS = 128
NB = 16
PAIRS = 12
CS = 4
CYCLE = 16
GROUP = 2
BLOCKS = 512


def with_ends(entries, rng, least, top_value):
    shape = entries.shape
    spot = [jax.random.randint(jax.random.fold_in(rng, axis), (), 0, shape[axis]) for axis in range(len(shape))]
    entries = entries.at[tuple(spot)].set(least)
    longest = shape.index(max(shape))
    spot[longest] = (spot[longest] + 1) % shape[longest]
    return entries.at[tuple(spot)].set(top_value)


def shard_levels(stream_key, dims, split, least, largest):
    gain = 1.0
    for dim, parts in split:
        draws = jax.random.uniform(jax.random.fold_in(jax.random.fold_in(stream_key, 6), dim), (parts,), jnp.float32, least / len(split), largest / len(split))
        gain = gain * jnp.repeat(jnp.exp(draws), dims[dim] // parts).reshape((-1,) + (1,) * (len(dims) - 1 - dim))
    return gain


def gaussian(stream_key, dims, spread, most, split=(), kind=jnp.bfloat16):
    entries = jax.random.normal(stream_key, dims, jnp.float32) * spread
    if len(split) > 0:
        entries = shard_levels(stream_key, dims, split, -0.22, 0.18) * entries
    return jnp.clip(entries, min=-most, max=most).astype(kind)


def setup_inputs(seed: int = 0) -> dict:
    arg_keys = jax.random.split(jax.random.key(seed), 5)
    x_blocks = gaussian(arg_keys[0], (BLOCKS, BS, BS), 0.1, 0.59765625, ((0, 32),))
    pair_left = with_ends(jax.random.randint(arg_keys[1], (CYCLE, GROUP, CYCLE, PAIRS), 0, GROUP * NB), jax.random.fold_in(arg_keys[1], 1), 0, (GROUP * NB) - 1).astype(jnp.int32)
    pair_right = with_ends(jax.random.randint(arg_keys[2], (CYCLE, GROUP, CYCLE, PAIRS), 0, GROUP * NB), jax.random.fold_in(arg_keys[2], 1), 0, (GROUP * NB) - 1).astype(jnp.int32)
    pair_target = with_ends(jax.random.randint(arg_keys[3], (CYCLE, GROUP, CYCLE, PAIRS), 0, CS), jax.random.fold_in(arg_keys[3], 1), 0, CS - 1).astype(jnp.int32)
    return {"x_blocks": x_blocks, "pair_left": pair_left, "pair_right": pair_right, "pair_target": pair_target}


def member_terms(gathered, left_index, right_index, target_index):
    left_tiles = jnp.take(gathered, left_index, axis=0).astype(jnp.float32)
    right_tiles = jnp.take(gathered, right_index, axis=0).astype(jnp.float32)
    product = jnp.einsum("spxy,spxz->spyz", left_tiles, right_tiles, precision=lax.Precision.HIGHEST)
    selector = (target_index[:, :, None] == jnp.arange(CS, dtype=jnp.int32)[None, None, :]).astype(jnp.float32)
    return jnp.einsum("spc,spyz->scyz", selector, product, precision=lax.Precision.HIGHEST)


def reference(x_blocks, pair_left, pair_right, pair_target):
    span = GROUP * NB
    visit_ids = jnp.arange(CYCLE, dtype=jnp.int32)

    def visit(summed, group_id):
        gathered = lax.dynamic_slice_in_dim(x_blocks, (group_id * span).astype(jnp.int32), span, 0)
        left_index = lax.dynamic_index_in_dim(pair_left, group_id, 0, keepdims=False)
        right_index = lax.dynamic_index_in_dim(pair_right, group_id, 0, keepdims=False)
        target_index = lax.dynamic_index_in_dim(pair_target, group_id, 0, keepdims=False)

        def per_member(items):
            return member_terms(gathered, items[0], items[1], items[2])

        contrib = lax.map(per_member, (left_index, right_index, target_index))
        owners = ((group_id - 1 - visit_ids) % CYCLE).astype(jnp.int32)
        summed = summed.at[owners].add(jnp.swapaxes(contrib, 0, 1))
        return summed, None

    start_sum = jnp.zeros((CYCLE, GROUP, CS, BS, BS), jnp.float32)
    summed, _ = lax.scan(visit, start_sum, jnp.arange(CYCLE, dtype=jnp.int32))
    return summed.astype(jnp.bfloat16)
```

```python
import functools

import jax
import jax.numpy as jnp
from jax import lax
from jax.experimental import pallas as pl
from jax.experimental.pallas import tpu as pltpu
from jax.sharding import PartitionSpec as P

CS = 4
PLANE = 4
STEPS = 32700.0
FINE = 64.0
MESH = pl.DeviceIdType.MESH


def kernel(
    n, g, nb, bs, pairs,
    x_ref, left_ref, right_ref, target_ref, out_ref,
    panel, panel_t, prods, part, own, send1, recv1, send2, recv2,
    gather_send, gather_recv, sem_s1, sem_r1, sem_s2, sem_r2,
):
    planes = n // PLANE
    me = lax.axis_index("blk")
    q = lax.axis_index("grp")
    hi, lo = me // PLANE, me % PLANE
    body_rows = CS * bs

    def far(k):
        return (hi ^ k) * PLANE + lo

    def near(j):
        return hi * PLANE + (lo ^ j)

    barrier = pltpu.get_barrier_semaphore()
    for d in range(1, g):
        pl.semaphore_signal(barrier, inc=1, device_id=(me, (q + d) % g), device_id_type=MESH)
    for j in range(1, PLANE):
        pl.semaphore_signal(barrier, inc=1, device_id=(near(j), q), device_id_type=MESH)
    for k in range(1, planes):
        pl.semaphore_signal(barrier, inc=1, device_id=(far(k), q), device_id_type=MESH)
    pl.semaphore_wait(barrier, (g - 1) + (PLANE - 1) + (planes - 1))

    gathers = []
    for d in range(1, g):
        copy = pltpu.make_async_remote_copy(
            src_ref=x_ref,
            dst_ref=panel.at[pl.ds(q * nb, nb)],
            send_sem=gather_send.at[d - 1],
            recv_sem=gather_recv.at[d - 1],
            device_id=(me, (q + d) % g),
            device_id_type=MESH,
        )
        copy.start()
        gathers.append(copy)

    def take_own(i, _):
        block = x_ref[i]
        panel[q * nb + i] = block
        panel_t[q * nb + i] = block.T
        return 0

    lax.fori_loop(0, nb, take_own, 0)
    for d in range(1, g):
        gathers[d - 1].wait_recv()
        source = (q - d + g) % g

        def take_other(i, _):
            panel_t[source * nb + i] = panel[source * nb + i].T
            return 0

        lax.fori_loop(0, nb, take_other, 0)

    def partial_sum(owner, put):
        s = (me - 1 - owner + 2 * n) % n
        for p in range(pairs):
            prods[p] = jnp.dot(
                panel_t[left_ref[s, p]],
                panel[right_ref[s, p]],
                preferred_element_type=jnp.float32,
            )
        masks = [
            [jnp.where(target_ref[s, p] == c, 1.0, 0.0) for c in range(CS)] for p in range(pairs)
        ]
        strip = 16
        for i in range(bs // strip):
            rows = pl.ds(i * strip, strip)
            totals = [None] * CS
            for p in range(pairs):
                value = prods[p, rows, :]
                for c in range(CS):
                    term = value * masks[p][c]
                    totals[c] = term if totals[c] is None else totals[c] + term
            for c in range(CS):
                put(c, rows, totals[c])

    def encode(c, value, dst):
        most = jnp.max(jnp.abs(value), axis=0, keepdims=True)
        level = jnp.ceil(jnp.log(jnp.maximum(most, 1e-30)) * FINE) + 1.0
        inverse = jnp.exp(level * (-1.0 / FINE)) * STEPS
        coded = jnp.round(value * inverse).astype(jnp.int32).astype(jnp.int16)
        dst[pl.ds(c * bs, bs), :] = coded
        return level

    def put_levels(levels, dst):
        row = lax.broadcasted_iota(jnp.int32, (16, bs), 0)
        table = jnp.zeros((16, bs), jnp.float32)
        for c in range(CS):
            table = jnp.where(row == c, levels[c], table)
        dst[pl.ds(body_rows, 16), :] = table.astype(jnp.int32).astype(jnp.int16)

    def get_scales(src):
        level = src[pl.ds(body_rows, 16), :].astype(jnp.int32).astype(jnp.float32)
        return jnp.exp(level * (1.0 / FINE)) * (1.0 / STEPS)

    def decode(c, scales, src):
        value = src[pl.ds(c * bs, bs), :].astype(jnp.int32).astype(jnp.float32)
        return value * scales[c : c + 1, :]

    def copy1(t, j):
        return pltpu.make_async_remote_copy(
            src_ref=send1.at[t, j - 1],
            dst_ref=recv1.at[t, j - 1],
            send_sem=sem_s1.at[t, j - 1],
            recv_sem=sem_r1.at[t, j - 1],
            device_id=(near(j), q),
            device_id_type=MESH,
        )

    def copy2(t):
        return pltpu.make_async_remote_copy(
            src_ref=send2.at[t],
            dst_ref=recv2.at[t],
            send_sem=sem_s2.at[t],
            recv_sem=sem_r2.at[t],
            device_id=(far(t + 1), q),
            device_id_type=MESH,
        )

    def compute(t):
        base = (hi ^ ((t + 1) % planes)) * PLANE

        def put_part(c, rows, value):
            part[c, rows, :] = value

        def one(j, _):
            partial_sum(base + (lo ^ j), put_part)
            dst = send1.at[t, j - 1]
            put_levels([encode(c, part[c], dst) for c in range(CS)], dst)
            copy1(t, j).start()
            return 0

        lax.fori_loop(1, PLANE, one, 0)

        def put_own(c, rows, value):
            own[t, c, rows, :] = value

        partial_sum(base + lo, put_own)

    def plane_total(t):
        for j in range(1, PLANE):
            copy1(t, j).wait_recv()
        scales = [get_scales(recv1.at[t, j]) for j in range(PLANE - 1)]
        for c in range(CS):
            value = own[t, c]
            for j in range(PLANE - 1):
                value = value + decode(c, scales[j], recv1.at[t, j])
            yield c, value

    def pass_on(t):
        dst = send2.at[t]
        put_levels([encode(c, value, dst) for c, value in plane_total(t)], dst)
        copy2(t).start()

    lag = 2

    def turn(t, _):
        @pl.when(t < planes)
        def _():
            compute(t)

        @pl.when(t >= lag)
        def _():
            pass_on(t - lag)

        return 0

    lax.fori_loop(0, planes - 1 + lag, turn, 0)

    last = planes - 1
    totals = [value for _, value in plane_total(last)]
    for c in range(CS):
        own[last, c] = totals[c]
    for t in range(last):
        copy2(t).wait_recv()
    scales = [get_scales(recv2.at[t]) for t in range(last)]
    for c in range(CS):
        value = own[last, c]
        for t in range(last):
            value = value + decode(c, scales[t], recv2.at[t])
        out_ref[c] = value.astype(jnp.bfloat16)

    for copy in gathers:
        copy.wait_send()

    def finish(t, _):
        for j in range(1, PLANE):
            copy1(t, j).wait_send()
        return 0

    lax.fori_loop(0, planes, finish, 0)
    for t in range(last):
        copy2(t).wait_send()


def per_device(x_blocks, pair_left, pair_right, pair_target):
    n = lax.axis_size("blk")
    g = lax.axis_size("grp")
    nb, bs = x_blocks.shape[0], x_blocks.shape[1]
    pairs = pair_left.shape[3]
    planes = n // PLANE
    message = CS * bs + 16
    vmem = pl.BlockSpec(memory_space=pltpu.VMEM)
    smem = pl.BlockSpec(memory_space=pltpu.SMEM)
    dma = pltpu.SemaphoreType.DMA
    out = pl.pallas_call(
        functools.partial(kernel, n, g, nb, bs, pairs),
        out_shape=jax.ShapeDtypeStruct((CS, bs, bs), jnp.bfloat16),
        in_specs=[vmem, smem, smem, smem],
        out_specs=vmem,
        scratch_shapes=[
            pltpu.VMEM((g * nb, bs, bs), jnp.bfloat16),
            pltpu.VMEM((g * nb, bs, bs), jnp.bfloat16),
            pltpu.VMEM((pairs, bs, bs), jnp.float32),
            pltpu.VMEM((CS, bs, bs), jnp.float32),
            pltpu.VMEM((planes, CS, bs, bs), jnp.float32),
            pltpu.VMEM((planes, PLANE - 1, message, bs), jnp.int16),
            pltpu.VMEM((planes, PLANE - 1, message, bs), jnp.int16),
            pltpu.VMEM((planes - 1, message, bs), jnp.int16),
            pltpu.VMEM((planes - 1, message, bs), jnp.int16),
            dma((g - 1,)),
            dma((g - 1,)),
            dma((planes, PLANE - 1)),
            dma((planes, PLANE - 1)),
            dma((planes - 1,)),
            dma((planes - 1,)),
        ],
        compiler_params=pltpu.CompilerParams(
            collective_id=0, has_side_effects=True, vmem_limit_bytes=48 * 1024 * 1024
        ),
    )(x_blocks, pair_left[0, 0], pair_right[0, 0], pair_target[0, 0])
    return out.reshape(1, 1, CS, bs, bs)


def solution(mesh):
    return jax.shard_map(
        per_device,
        mesh=mesh,
        in_specs=(
            P(("blk", "grp"), None, None),
            P("blk", "grp", None, None),
            P("blk", "grp", None, None),
            P("blk", "grp", None, None),
        ),
        out_specs=P("blk", "grp", None, None, None),
        check_vma=False,
    )
```

```python
import functools

import jax
import jax.numpy as jnp
from jax import lax
from jax.experimental import pallas as pl
from jax.experimental.pallas import tpu as pltpu
from jax.sharding import PartitionSpec as P

CS = 4
PLANE = 4
HALF = CS // 2
STEPS = 32700.0
FINE = 64.0
MESH = pl.DeviceIdType.MESH


def kernel(
    n, g, nb, bs, pairs,
    x_ref, left_ref, right_ref, target_ref, out_ref,
    panel, panel_t, prods, acc, send_a, recv_a, send_b, recv_b, send2, recv2,
    gather_send, gather_recv, sem_sa, sem_ra, sem_sb, sem_rb, sem_s2, sem_r2,
):
    planes = n // PLANE
    me = lax.axis_index("blk")
    q = lax.axis_index("grp")
    hi, lo = me // PLANE, me % PLANE

    def far(k):
        return (hi ^ k) * PLANE + lo

    def near(j):
        return hi * PLANE + (lo ^ j)

    barrier = pltpu.get_barrier_semaphore()
    for d in range(1, g):
        pl.semaphore_signal(barrier, inc=1, device_id=(me, (q + d) % g), device_id_type=MESH)
    for j in (1, 2):
        pl.semaphore_signal(barrier, inc=1, device_id=(near(j), q), device_id_type=MESH)
    for k in range(1, planes):
        pl.semaphore_signal(barrier, inc=1, device_id=(far(k), q), device_id_type=MESH)
    pl.semaphore_wait(barrier, (g - 1) + 2 + (planes - 1))

    gathers = []
    for d in range(1, g):
        copy = pltpu.make_async_remote_copy(
            src_ref=x_ref,
            dst_ref=panel.at[pl.ds(q * nb, nb)],
            send_sem=gather_send.at[d - 1],
            recv_sem=gather_recv.at[d - 1],
            device_id=(me, (q + d) % g),
            device_id_type=MESH,
        )
        copy.start()
        gathers.append(copy)

    def take_own(i, _):
        block = x_ref[i]
        panel[q * nb + i] = block
        panel_t[q * nb + i] = block.T
        return 0

    lax.fori_loop(0, nb, take_own, 0)
    for d in range(1, g):
        gathers[d - 1].wait_recv()
        source = (q - d + g) % g

        def take_other(i, _):
            panel_t[source * nb + i] = panel[source * nb + i].T
            return 0

        lax.fori_loop(0, nb, take_other, 0)

    def partial_sum(t, m):
        owner = (hi ^ ((t + 1) % planes)) * PLANE + (lo ^ m)
        s = (me - 1 - owner + 2 * n) % n
        for p in range(pairs):
            prods[p] = jnp.dot(
                panel_t[left_ref[s, p]],
                panel[right_ref[s, p]],
                preferred_element_type=jnp.float32,
            )
        masks = [
            [jnp.where(target_ref[s, p] == c, 1.0, 0.0) for c in range(CS)] for p in range(pairs)
        ]
        strip = 16
        for i in range(bs // strip):
            rows = pl.ds(i * strip, strip)
            totals = [None] * CS
            for p in range(pairs):
                value = prods[p, rows, :]
                for c in range(CS):
                    term = value * masks[p][c]
                    totals[c] = term if totals[c] is None else totals[c] + term
            for c in range(CS):
                acc[t, m, c, rows, :] = totals[c]

    def encode(values, dst):
        row = lax.broadcasted_iota(jnp.int32, (16, bs), 0)
        table = jnp.zeros((16, bs), jnp.float32)
        for i, value in enumerate(values):
            most = jnp.max(jnp.abs(value), axis=0, keepdims=True)
            level = jnp.ceil(jnp.log(jnp.maximum(most, 1e-30)) * FINE) + 1.0
            inverse = jnp.exp(level * (-1.0 / FINE)) * STEPS
            coded = jnp.round(value * inverse).astype(jnp.int32).astype(jnp.int16)
            dst[pl.ds(i * bs, bs), :] = coded
            table = jnp.where(row == i, level, table)
        dst[pl.ds(len(values) * bs, 16), :] = table.astype(jnp.int32).astype(jnp.int16)

    def decode(count, src):
        level = src[pl.ds(count * bs, 16), :].astype(jnp.int32).astype(jnp.float32)
        scales = jnp.exp(level * (1.0 / FINE)) * (1.0 / STEPS)

        def block(i):
            value = src[pl.ds(i * bs, bs), :].astype(jnp.int32).astype(jnp.float32)
            return value * scales[i : i + 1, :]

        return block

    def copy_a(t, h, a):
        return pltpu.make_async_remote_copy(
            src_ref=send_a.at[t, h, a],
            dst_ref=recv_a.at[t, h, a],
            send_sem=sem_sa.at[t, h, a],
            recv_sem=sem_ra.at[t, h, a],
            device_id=(near(1 + h), q),
            device_id_type=MESH,
        )

    def copy_b(t, h):
        return pltpu.make_async_remote_copy(
            src_ref=send_b.at[t, h],
            dst_ref=recv_b.at[t, h],
            send_sem=sem_sb.at[t, h],
            recv_sem=sem_rb.at[t, h],
            device_id=(near(2 - h), q),
            device_id_type=MESH,
        )

    def copy2(t):
        return pltpu.make_async_remote_copy(
            src_ref=send2.at[t],
            dst_ref=recv2.at[t],
            send_sem=sem_s2.at[t],
            recv_sem=sem_r2.at[t],
            device_id=(far(t + 1), q),
            device_id_type=MESH,
        )

    def compute(t):
        def one(j, _):
            m = PLANE - 1 - j
            partial_sum(t, m)

            def send(h, a):
                encode([acc[t, m, HALF * h + i] for i in range(HALF)], send_a.at[t, h, a])
                copy_a(t, h, a).start()

            @pl.when(m == PLANE - 1)
            def _():
                for h in range(2):
                    send(h, 0)

            @pl.when((m == 1) | (m == 2))
            def _():
                send(m - 1, 1)

            return 0

        lax.fori_loop(0, PLANE, one, 0)

    def turn_corner(t):
        for h in range(2):
            copy_a(t, h, 0).wait_recv()
            came = decode(HALF, recv_a.at[t, h, 0])
            encode(
                [acc[t, 2 - h, HALF * h + i] + came(i) for i in range(HALF)], send_b.at[t, h]
            )
            copy_b(t, h).start()

    def plane_total(t):
        for h in range(2):
            copy_a(t, h, 1).wait_recv()
            copy_b(t, h).wait_recv()
            first = decode(HALF, recv_a.at[t, h, 1])
            second = decode(HALF, recv_b.at[t, h])
            for i in range(HALF):
                acc[t, 0, HALF * h + i] = acc[t, 0, HALF * h + i] + first(i) + second(i)

    def pass_on(t):
        plane_total(t)
        encode([acc[t, 0, c] for c in range(CS)], send2.at[t])
        copy2(t).start()

    last = planes - 1

    def turn(t, _):
        @pl.when(t < planes)
        def _():
            compute(t)

        @pl.when((t >= 1) & (t < planes + 1))
        def _():
            turn_corner(t - 1)

        @pl.when(t >= 2)
        def _():
            pass_on(t - 2)

        return 0

    lax.fori_loop(0, last + 2, turn, 0)

    plane_total(last)
    for t in range(last):
        copy2(t).wait_recv()
    came = [decode(CS, recv2.at[t]) for t in range(last)]
    for c in range(CS):
        value = acc[last, 0, c]
        for t in range(last):
            value = value + came[t](c)
        out_ref[c] = value.astype(jnp.bfloat16)

    for copy in gathers:
        copy.wait_send()

    def finish(t, _):
        for h in range(2):
            for a in range(2):
                copy_a(t, h, a).wait_send()
            copy_b(t, h).wait_send()
        return 0

    lax.fori_loop(0, planes, finish, 0)
    for t in range(last):
        copy2(t).wait_send()


def per_device(x_blocks, pair_left, pair_right, pair_target):
    n = lax.axis_size("blk")
    g = lax.axis_size("grp")
    nb, bs = x_blocks.shape[0], x_blocks.shape[1]
    pairs = pair_left.shape[3]
    planes = n // PLANE
    message = CS * bs + 16
    short = HALF * bs + 16
    vmem = pl.BlockSpec(memory_space=pltpu.VMEM)
    smem = pl.BlockSpec(memory_space=pltpu.SMEM)
    dma = pltpu.SemaphoreType.DMA
    out = pl.pallas_call(
        functools.partial(kernel, n, g, nb, bs, pairs),
        out_shape=jax.ShapeDtypeStruct((CS, bs, bs), jnp.bfloat16),
        in_specs=[vmem, smem, smem, smem],
        out_specs=vmem,
        scratch_shapes=[
            pltpu.VMEM((g * nb, bs, bs), jnp.bfloat16),
            pltpu.VMEM((g * nb, bs, bs), jnp.bfloat16),
            pltpu.VMEM((pairs, bs, bs), jnp.float32),
            pltpu.VMEM((planes, PLANE, CS, bs, bs), jnp.float32),
            pltpu.VMEM((planes, 2, 2, short, bs), jnp.int16),
            pltpu.VMEM((planes, 2, 2, short, bs), jnp.int16),
            pltpu.VMEM((planes, 2, short, bs), jnp.int16),
            pltpu.VMEM((planes, 2, short, bs), jnp.int16),
            pltpu.VMEM((planes - 1, message, bs), jnp.int16),
            pltpu.VMEM((planes - 1, message, bs), jnp.int16),
            dma((g - 1,)),
            dma((g - 1,)),
            dma((planes, 2, 2)),
            dma((planes, 2, 2)),
            dma((planes, 2)),
            dma((planes, 2)),
            dma((planes - 1,)),
            dma((planes - 1,)),
        ],
        compiler_params=pltpu.CompilerParams(
            collective_id=0, has_side_effects=True, vmem_limit_bytes=48 * 1024 * 1024
        ),
    )(x_blocks, pair_left[0, 0], pair_right[0, 0], pair_target[0, 0])
    return out.reshape(1, 1, CS, bs, bs)


def solution(mesh):
    return jax.shard_map(
        per_device,
        mesh=mesh,
        in_specs=(
            P(("blk", "grp"), None, None),
            P("blk", "grp", None, None),
            P("blk", "grp", None, None),
            P("blk", "grp", None, None),
        ),
        out_specs=P("blk", "grp", None, None, None),
        check_vma=False,
    )
```

```python
import functools

import jax
import jax.numpy as jnp
from jax import lax
from jax.experimental import pallas as pl
from jax.experimental.pallas import tpu as pltpu
from jax.sharding import PartitionSpec as P

CS = 4
PLANE = 4
HALF = CS // 2
STEPS = 32700.0
FINE = 64.0
MESH = pl.DeviceIdType.MESH


def kernel(
    n, g, nb, bs, pairs,
    x_ref, left_ref, right_ref, target_ref, out_ref,
    panel, panel_t, prods, acc, send_a, recv_a, send_b, recv_b, send2, recv2,
    gather_own, gather_send, gather_recv, sem_sa, sem_ra, sem_sb, sem_rb, sem_s2, sem_r2,
):
    planes = n // PLANE
    me = lax.axis_index("blk")
    q = lax.axis_index("grp")
    hi, lo = me // PLANE, me % PLANE

    def far(k):
        return (hi ^ k) * PLANE + lo

    def near(j):
        return hi * PLANE + (lo ^ j)

    held = pltpu.make_async_copy(x_ref, panel.at[pl.ds(q * nb, nb)], gather_own)
    held.start()
    barrier = pltpu.get_barrier_semaphore()
    for d in range(1, g):
        pl.semaphore_signal(barrier, inc=1, device_id=(me, (q + d) % g), device_id_type=MESH)
    for j in (1, 2):
        pl.semaphore_signal(barrier, inc=1, device_id=(near(j), q), device_id_type=MESH)
    for k in range(1, planes):
        pl.semaphore_signal(barrier, inc=1, device_id=(far(k), q), device_id_type=MESH)
    pl.semaphore_wait(barrier, (g - 1) + 2 + (planes - 1))

    gathers = []
    for d in range(1, g):
        copy = pltpu.make_async_remote_copy(
            src_ref=x_ref,
            dst_ref=panel.at[pl.ds(q * nb, nb)],
            send_sem=gather_send.at[d - 1],
            recv_sem=gather_recv.at[d - 1],
            device_id=(me, (q + d) % g),
            device_id_type=MESH,
        )
        copy.start()
        gathers.append(copy)

    def take_own(i, _):
        panel_t[q * nb + i] = panel[q * nb + i].T
        return 0

    held.wait()
    lax.fori_loop(0, nb, take_own, 0)
    for d in range(1, g):
        gathers[d - 1].wait_recv()
        source = (q - d + g) % g

        def take_other(i, _):
            panel_t[source * nb + i] = panel[source * nb + i].T
            return 0

        lax.fori_loop(0, nb, take_other, 0)

    def partial_sum(t, m):
        owner = (hi ^ (planes - 1 - t)) * PLANE + (lo ^ m)
        s = (me - 1 - owner + 2 * n) % n
        for p in range(pairs):
            prods[p] = jnp.dot(
                panel_t[left_ref[p, 0, s]],
                panel[right_ref[p, 0, s]],
                preferred_element_type=jnp.float32,
            )
        masks = [
            [jnp.where(target_ref[p, 0, s] == c, 1.0, 0.0) for c in range(CS)] for p in range(pairs)
        ]
        strip = 16
        for i in range(bs // strip):
            rows = pl.ds(i * strip, strip)
            totals = [None] * CS
            for p in range(pairs):
                value = prods[p, rows, :]
                for c in range(CS):
                    term = value * masks[p][c]
                    totals[c] = term if totals[c] is None else totals[c] + term
            for c in range(CS):
                acc[t, m, c, rows, :] = totals[c]

    def encode(values, dst):
        row = lax.broadcasted_iota(jnp.int32, (16, bs), 0)
        table = jnp.zeros((16, bs), jnp.float32)
        for i, value in enumerate(values):
            most = jnp.max(jnp.abs(value), axis=0, keepdims=True)
            level = jnp.ceil(jnp.log(jnp.maximum(most, 1e-30)) * FINE) + 1.0
            inverse = jnp.exp(level * (-1.0 / FINE)) * STEPS
            coded = jnp.round(value * inverse).astype(jnp.int32).astype(jnp.int16)
            dst[pl.ds(i * bs, bs), :] = coded
            table = jnp.where(row == i, level, table)
        dst[pl.ds(len(values) * bs, 16), :] = table.astype(jnp.int32).astype(jnp.int16)

    def decode(count, src):
        level = src[pl.ds(count * bs, 16), :].astype(jnp.int32).astype(jnp.float32)
        scales = jnp.exp(level * (1.0 / FINE)) * (1.0 / STEPS)

        def block(i):
            value = src[pl.ds(i * bs, bs), :].astype(jnp.int32).astype(jnp.float32)
            return value * scales[i : i + 1, :]

        return block

    def copy_a(t, h, a):
        return pltpu.make_async_remote_copy(
            src_ref=send_a.at[t, h, a],
            dst_ref=recv_a.at[t, h, a],
            send_sem=sem_sa.at[t, h, a],
            recv_sem=sem_ra.at[t, h, a],
            device_id=(near(1 + h), q),
            device_id_type=MESH,
        )

    def copy_b(t, h):
        return pltpu.make_async_remote_copy(
            src_ref=send_b.at[t, h],
            dst_ref=recv_b.at[t, h],
            send_sem=sem_sb.at[t, h],
            recv_sem=sem_rb.at[t, h],
            device_id=(near(2 - h), q),
            device_id_type=MESH,
        )

    def copy2(t):
        return pltpu.make_async_remote_copy(
            src_ref=send2.at[t],
            dst_ref=recv2.at[t],
            send_sem=sem_s2.at[t],
            recv_sem=sem_r2.at[t],
            device_id=(far(planes - 1 - t), q),
            device_id_type=MESH,
        )

    def compute(t, begin, end):
        def one(j, _):
            m = PLANE - 1 - j
            partial_sum(t, m)

            def send(h, a):
                encode([acc[t, m, HALF * h + i] for i in range(HALF)], send_a.at[t, h, a])
                copy_a(t, h, a).start()

            @pl.when(m == PLANE - 1)
            def _():
                for h in range(2):
                    send(h, 0)

            @pl.when((m == 1) | (m == 2))
            def _():
                send(m - 1, 1)

            return 0

        lax.fori_loop(begin, end, one, 0)

    def turn_corner(t):
        for h in range(2):
            copy_a(t, h, 0).wait_recv()
            came = decode(HALF, recv_a.at[t, h, 0])
            encode(
                [acc[t, 2 - h, HALF * h + i] + came(i) for i in range(HALF)], send_b.at[t, h]
            )
            copy_b(t, h).start()

    def plane_total(t):
        for h in range(2):
            copy_a(t, h, 1).wait_recv()
            copy_b(t, h).wait_recv()
            first = decode(HALF, recv_a.at[t, h, 1])
            second = decode(HALF, recv_b.at[t, h])
            for i in range(HALF):
                acc[t, 0, HALF * h + i] = acc[t, 0, HALF * h + i] + first(i) + second(i)

    def pass_on(t):
        plane_total(t)
        encode([acc[t, 0, c] for c in range(CS)], send2.at[t])
        copy2(t).start()

    last = planes - 1

    def turn(t, _):
        @pl.when(t < planes)
        def _():
            compute(t, 0, 1)

        @pl.when((t >= 1) & (t < planes + 1))
        def _():
            turn_corner(t - 1)

        @pl.when(t < planes)
        def _():
            compute(t, 1, PLANE)

        @pl.when(t >= 2)
        def _():
            pass_on(t - 2)

        return 0

    lax.fori_loop(0, last + 2, turn, 0)

    plane_total(last)
    for t in range(last):
        copy2(t).wait_recv()
    came = [decode(CS, recv2.at[t]) for t in range(last)]
    for c in range(CS):
        value = acc[last, 0, c]
        for t in range(last):
            value = value + came[t](c)
        out_ref[c] = value.astype(jnp.bfloat16)

    for copy in gathers:
        copy.wait_send()

    def finish(t, _):
        for h in range(2):
            for a in range(2):
                copy_a(t, h, a).wait_send()
            copy_b(t, h).wait_send()
        return 0

    lax.fori_loop(0, planes, finish, 0)
    for t in range(last):
        copy2(t).wait_send()


def per_device(x_blocks, pair_left, pair_right, pair_target):
    n = lax.axis_size("blk")
    g = lax.axis_size("grp")
    nb, bs = x_blocks.shape[0], x_blocks.shape[1]
    pairs = pair_left.shape[3]
    planes = n // PLANE
    message = CS * bs + 16
    short = HALF * bs + 16
    vmem = pl.BlockSpec(memory_space=pltpu.VMEM)
    smem = pl.BlockSpec(memory_space=pltpu.SMEM)
    dma = pltpu.SemaphoreType.DMA
    tables = [jnp.transpose(a[0], (2, 0, 1)) for a in (pair_left, pair_right, pair_target)]
    out = pl.pallas_call(
        functools.partial(kernel, n, g, nb, bs, pairs),
        out_shape=jax.ShapeDtypeStruct((CS, bs, bs), jnp.bfloat16),
        in_specs=[pl.BlockSpec(memory_space=pltpu.HBM), smem, smem, smem],
        out_specs=vmem,
        scratch_shapes=[
            pltpu.VMEM((g * nb, bs, bs), jnp.bfloat16),
            pltpu.VMEM((g * nb, bs, bs), jnp.bfloat16),
            pltpu.VMEM((pairs, bs, bs), jnp.float32),
            pltpu.VMEM((planes, PLANE, CS, bs, bs), jnp.float32),
            pltpu.VMEM((planes, 2, 2, short, bs), jnp.int16),
            pltpu.VMEM((planes, 2, 2, short, bs), jnp.int16),
            pltpu.VMEM((planes, 2, short, bs), jnp.int16),
            pltpu.VMEM((planes, 2, short, bs), jnp.int16),
            pltpu.VMEM((planes - 1, message, bs), jnp.int16),
            pltpu.VMEM((planes - 1, message, bs), jnp.int16),
            dma,
            dma((g - 1,)),
            dma((g - 1,)),
            dma((planes, 2, 2)),
            dma((planes, 2, 2)),
            dma((planes, 2)),
            dma((planes, 2)),
            dma((planes - 1,)),
            dma((planes - 1,)),
        ],
        compiler_params=pltpu.CompilerParams(
            collective_id=0, has_side_effects=True, vmem_limit_bytes=64 * 1024 * 1024
        ),
    )(x_blocks, *tables)
    return out.reshape(1, 1, CS, bs, bs)


def solution(mesh):
    return jax.shard_map(
        per_device,
        mesh=mesh,
        in_specs=(
            P(("blk", "grp"), None, None),
            P("blk", "grp", None, None),
            P("blk", "grp", None, None),
            P("blk", "grp", None, None),
        ),
        out_specs=P("blk", "grp", None, None, None),
        check_vma=False,
    )
```

```python
import functools

import jax
import jax.numpy as jnp
from jax import lax
from jax.experimental import pallas as pl
from jax.experimental.pallas import tpu as pltpu
from jax.sharding import PartitionSpec as P

CS = 4
PLANE = 4
BESIDE = 1
HALF = CS // 2
STEPS = 32700.0
FINE = 64.0
MESH = pl.DeviceIdType.MESH


def kernel(
    n, g, nb, bs, pairs,
    x_ref, left_ref, right_ref, target_ref, out_ref,
    panel, panel_t, prods, acc, send_a, recv_a, send_b, recv_b, send2, recv2,
    gather_own, gather_send, gather_recv, sem_sa, sem_ra, sem_sb, sem_rb, sem_s2, sem_r2,
):
    planes = n // PLANE
    me = lax.axis_index("blk")
    q = lax.axis_index("grp")
    hi, lo = me // PLANE, me % PLANE

    def far(k):
        return (hi ^ k) * PLANE + lo

    def near(j):
        return hi * PLANE + (lo ^ j)

    held = pltpu.make_async_copy(x_ref, panel.at[pl.ds(q * nb, nb)], gather_own)
    held.start()
    barrier = pltpu.get_barrier_semaphore()
    for d in range(1, g):
        pl.semaphore_signal(barrier, inc=1, device_id=(me, (q + d) % g), device_id_type=MESH)
    for j in (1, 2):
        pl.semaphore_signal(barrier, inc=1, device_id=(near(j), q), device_id_type=MESH)
    for k in range(1, planes):
        pl.semaphore_signal(barrier, inc=1, device_id=(far(k), q), device_id_type=MESH)
    pl.semaphore_wait(barrier, (g - 1) + 2 + (planes - 1))

    gathers = []
    for d in range(1, g):
        copy = pltpu.make_async_remote_copy(
            src_ref=x_ref,
            dst_ref=panel.at[pl.ds(q * nb, nb)],
            send_sem=gather_send.at[d - 1],
            recv_sem=gather_recv.at[d - 1],
            device_id=(me, (q + d) % g),
            device_id_type=MESH,
        )
        copy.start()
        gathers.append(copy)

    def take_own(i, _):
        panel_t[q * nb + i] = panel[q * nb + i].T
        return 0

    held.wait()
    lax.fori_loop(0, nb, take_own, 0)
    for d in range(1, g):
        gathers[d - 1].wait_recv()
        source = (q - d + g) % g

        def take_other(i, _):
            panel_t[source * nb + i] = panel[source * nb + i].T
            return 0

        lax.fori_loop(0, nb, take_other, 0)

    last = planes - 1

    def plane_of(t):
        inner = jnp.where(t == BESIDE, 1, planes - t - jnp.where(t == 0, 1, 0))
        return jnp.where(t == last, 0, inner)

    def partial_sum(t, m):
        owner = (hi ^ plane_of(t)) * PLANE + (lo ^ m)
        s = (me - 1 - owner + 2 * n) % n
        for p in range(pairs):
            prods[p] = jnp.dot(
                panel_t[left_ref[p, 0, s]],
                panel[right_ref[p, 0, s]],
                preferred_element_type=jnp.float32,
            )
        masks = [
            [jnp.where(target_ref[p, 0, s] == c, 1.0, 0.0) for c in range(CS)] for p in range(pairs)
        ]
        strip = 16
        for i in range(bs // strip):
            rows = pl.ds(i * strip, strip)
            totals = [None] * CS
            for p in range(pairs):
                value = prods[p, rows, :]
                for c in range(CS):
                    term = value * masks[p][c]
                    totals[c] = term if totals[c] is None else totals[c] + term
            for c in range(CS):
                acc[t, m, c, rows, :] = totals[c]

    def encode(values, dst):
        row = lax.broadcasted_iota(jnp.int32, (16, bs), 0)
        table = jnp.zeros((16, bs), jnp.float32)
        for i, value in enumerate(values):
            most = jnp.max(jnp.abs(value), axis=0, keepdims=True)
            level = jnp.ceil(jnp.log(jnp.maximum(most, 1e-30)) * FINE) + 1.0
            inverse = jnp.exp(level * (-1.0 / FINE)) * STEPS
            coded = jnp.round(value * inverse).astype(jnp.int32).astype(jnp.int16)
            dst[pl.ds(i * bs, bs), :] = coded
            table = jnp.where(row == i, level, table)
        dst[pl.ds(len(values) * bs, 16), :] = table.astype(jnp.int32).astype(jnp.int16)

    def decode(count, src):
        level = src[pl.ds(count * bs, 16), :].astype(jnp.int32).astype(jnp.float32)
        scales = jnp.exp(level * (1.0 / FINE)) * (1.0 / STEPS)

        def block(i):
            value = src[pl.ds(i * bs, bs), :].astype(jnp.int32).astype(jnp.float32)
            return value * scales[i : i + 1, :]

        return block

    def copy_a(t, h, a):
        return pltpu.make_async_remote_copy(
            src_ref=send_a.at[t, h, a],
            dst_ref=recv_a.at[t, h, a],
            send_sem=sem_sa.at[t, h, a],
            recv_sem=sem_ra.at[t, h, a],
            device_id=(jnp.where(t == BESIDE, far(1), near(1 + h)), q),
            device_id_type=MESH,
        )

    def copy_b(t, h):
        return pltpu.make_async_remote_copy(
            src_ref=send_b.at[t, h],
            dst_ref=recv_b.at[t, h],
            send_sem=sem_sb.at[t, h],
            recv_sem=sem_rb.at[t, h],
            device_id=(near(2 - h), q),
            device_id_type=MESH,
        )

    def copy2(t):
        return pltpu.make_async_remote_copy(
            src_ref=send2.at[t],
            dst_ref=recv2.at[t],
            send_sem=sem_s2.at[t],
            recv_sem=sem_r2.at[t],
            device_id=(far(plane_of(t)), q),
            device_id_type=MESH,
        )

    def compute(t, begin, end):
        def one(j, _):
            m = PLANE - 1 - j
            partial_sum(t, m)

            def send(h, a):
                @pl.when(t == last)
                def _():
                    copy_a(BESIDE, h, a).wait_recv()
                    came = decode(HALF, recv_a.at[BESIDE, h, a])
                    for i in range(HALF):
                        acc[t, m, HALF * h + i] = acc[t, m, HALF * h + i] + came(i)

                encode([acc[t, m, HALF * h + i] for i in range(HALF)], send_a.at[t, h, a])
                copy_a(t, h, a).start()

            @pl.when(m == PLANE - 1)
            def _():
                for h in range(2):
                    send(h, 0)

            @pl.when((m == 1) | (m == 2))
            def _():
                send(m - 1, 1)

            return 0

        lax.fori_loop(begin, end, one, 0)

    def turn_corner(t):
        for h in range(2):
            @pl.when(t != BESIDE)
            def _():
                copy_a(t, h, 0).wait_recv()
                came = decode(HALF, recv_a.at[t, h, 0])
                for i in range(HALF):
                    acc[t, 2 - h, HALF * h + i] = acc[t, 2 - h, HALF * h + i] + came(i)

            encode([acc[t, 2 - h, HALF * h + i] for i in range(HALF)], send_b.at[t, h])
            copy_b(t, h).start()

    def plane_total(t):
        for h in range(2):
            @pl.when(t != BESIDE)
            def _():
                copy_a(t, h, 1).wait_recv()
                first = decode(HALF, recv_a.at[t, h, 1])
                for i in range(HALF):
                    acc[t, 0, HALF * h + i] = acc[t, 0, HALF * h + i] + first(i)

            copy_b(t, h).wait_recv()
            second = decode(HALF, recv_b.at[t, h])
            for i in range(HALF):
                acc[t, 0, HALF * h + i] = acc[t, 0, HALF * h + i] + second(i)

    def pass_on(t):
        plane_total(t)
        encode([acc[t, 0, c] for c in range(CS)], send2.at[t])
        copy2(t).start()

    def turn(t, _):
        @pl.when(t < planes)
        def _():
            compute(t, 0, 1)

        @pl.when((t >= 1) & (t < planes + 1))
        def _():
            turn_corner(t - 1)

        @pl.when(t < planes)
        def _():
            compute(t, 1, PLANE)

        @pl.when(t >= 2)
        def _():
            pass_on(t - 2)

        return 0

    lax.fori_loop(0, last + 2, turn, 0)

    plane_total(last)
    for t in range(last):
        copy2(t).wait_recv()
    came = [decode(CS, recv2.at[t]) for t in range(last)]
    for c in range(CS):
        value = acc[last, 0, c]
        for t in range(last):
            value = value + came[t](c)
        out_ref[c] = value.astype(jnp.bfloat16)

    for copy in gathers:
        copy.wait_send()

    def finish(t, _):
        for h in range(2):
            for a in range(2):
                copy_a(t, h, a).wait_send()
            copy_b(t, h).wait_send()
        return 0

    lax.fori_loop(0, planes, finish, 0)
    for t in range(last):
        copy2(t).wait_send()


def per_device(x_blocks, pair_left, pair_right, pair_target):
    n = lax.axis_size("blk")
    g = lax.axis_size("grp")
    nb, bs = x_blocks.shape[0], x_blocks.shape[1]
    pairs = pair_left.shape[3]
    planes = n // PLANE
    message = CS * bs + 16
    short = HALF * bs + 16
    vmem = pl.BlockSpec(memory_space=pltpu.VMEM)
    smem = pl.BlockSpec(memory_space=pltpu.SMEM)
    dma = pltpu.SemaphoreType.DMA
    tables = [jnp.transpose(a[0], (2, 0, 1)) for a in (pair_left, pair_right, pair_target)]
    out = pl.pallas_call(
        functools.partial(kernel, n, g, nb, bs, pairs),
        out_shape=jax.ShapeDtypeStruct((CS, bs, bs), jnp.bfloat16),
        in_specs=[pl.BlockSpec(memory_space=pltpu.HBM), smem, smem, smem],
        out_specs=vmem,
        scratch_shapes=[
            pltpu.VMEM((g * nb, bs, bs), jnp.bfloat16),
            pltpu.VMEM((g * nb, bs, bs), jnp.bfloat16),
            pltpu.VMEM((pairs, bs, bs), jnp.float32),
            pltpu.VMEM((planes, PLANE, CS, bs, bs), jnp.float32),
            pltpu.VMEM((planes, 2, 2, short, bs), jnp.int16),
            pltpu.VMEM((planes, 2, 2, short, bs), jnp.int16),
            pltpu.VMEM((planes, 2, short, bs), jnp.int16),
            pltpu.VMEM((planes, 2, short, bs), jnp.int16),
            pltpu.VMEM((planes - 1, message, bs), jnp.int16),
            pltpu.VMEM((planes - 1, message, bs), jnp.int16),
            dma,
            dma((g - 1,)),
            dma((g - 1,)),
            dma((planes, 2, 2)),
            dma((planes, 2, 2)),
            dma((planes, 2)),
            dma((planes, 2)),
            dma((planes - 1,)),
            dma((planes - 1,)),
        ],
        compiler_params=pltpu.CompilerParams(
            collective_id=0, has_side_effects=True, vmem_limit_bytes=64 * 1024 * 1024
        ),
    )(x_blocks, *tables)
    return out.reshape(1, 1, CS, bs, bs)


def solution(mesh):
    return jax.shard_map(
        per_device,
        mesh=mesh,
        in_specs=(
            P(("blk", "grp"), None, None),
            P("blk", "grp", None, None),
            P("blk", "grp", None, None),
            P("blk", "grp", None, None),
        ),
        out_specs=P("blk", "grp", None, None, None),
        check_vma=False,
    )
```
